32 devices in a mesh: groups: 2 (over x), tm: 4 (over y, core), ingest: 4 (over z).
Axes of the slice: x: 2, y: 2, z: 4, core: 2. Of those that a mesh axis runs over, the one named last changes fastest.
Arguments:
- transition: float32 [512, 512], replicated, may hold values from -1.01 to 1.01
- gain: float32 [512, 512], replicated, may hold values from -0.01 to 0.21
- smoother_gain: float32 [512, 512], replicated, may hold values from -1.01 to 1.01
- start_state: float32 [1024], P('groups'), parts along dimension 0, may hold values from -6 to 6
- rows_float: float32 [6, 2, 32, 16], P(None, None, ('groups', 'tm', 'ingest')), parts along dimension 2, may hold values from -6 to 6, as said below
- rows_index: int32 [2, 2, 32, 16], P(None, None, ('groups', 'tm', 'ingest')), parts along dimension 2, may hold values from 0 to 127, as said below
Outputs:
- filtered: float32 [128, 512], P(('groups', 'tm', 'ingest')), parts along dimension 0
- smoothed: float32 [128, 512], P(('groups', 'tm', 'ingest')), parts along dimension 0
The draws below stay inside these ranges and needn't reach their ends.
There are 2 independent parts, one for each index of `groups`. The reference program is written for one: setup_inputs(seed, part) draws one part's arguments, and reference() takes and returns one part's arrays. A program takes and returns all parts, laid end to end along the dimension named above; an argument that names none is the same for every part. Nothing has to cross between parts.
Inputs may be any that keep to these rules, and one draw needn't show every extreme that they name: rows_index[0] is a step within the owner, or 4 for an empty slot; rows_index[1] is a state block below 128. rows_float[0] readings; rows_float[1] precisions between 0.5 and 2; rows_float[2] to rows_float[5] coefficients within -0.7 to 0.7.
All inputs are finite; a program needn't handle non-finite values.
Results may differ from the reference program's by a relative error of at most 0.0003.
Values sent between devices are 32-bit elements; how exact they have to be, the bound alone decides.
A program may use at most 128 MiB of HBM per device.

```python
import math
import jax
import jax.numpy as jnp
from jax import lax

STATE = 512
BLOCKS = 128
STEPS_DEV = 4
CAP = 2
DEVS = 16
TOTAL = 64


def rotation_blocks(base_key, slowest, fastest, spread_size):
    subkeys = jax.random.split(base_key, 3)
    halves = STATE // 2
    losses = jnp.exp(jax.random.uniform(subkeys[0], (halves,), jnp.float32, math.log(slowest), math.log(fastest)))
    magnitudes = 1.0 - losses
    angles = jax.random.uniform(subkeys[1], (halves,), jnp.float32, -0.3, 0.3)
    pair_ids = jnp.arange(STATE) // 2
    row_ids = jnp.arange(STATE)[:, None]
    col_ids = jnp.arange(STATE)[None, :]
    cosines = (magnitudes * jnp.cos(angles))[pair_ids][:, None]
    sines = (magnitudes * jnp.sin(angles))[pair_ids][:, None]
    same_pair = pair_ids[:, None] == pair_ids[None, :]
    rotated = jnp.where(row_ids == col_ids, cosines, jnp.where(row_ids % 2 == 0, -sines, sines))
    scatter_part = jax.random.uniform(subkeys[2], (STATE, STATE), jnp.float32, -spread_size, spread_size)
    return jnp.where(same_pair, rotated, 0.0) + scatter_part


def draw_transition(key, part):
    return rotation_blocks(jax.random.fold_in(key, 11), 0.5 / TOTAL, 0.05, 5e-05)


def draw_smoother_gain(key, part):
    return rotation_blocks(jax.random.fold_in(key, 22), 1.0 / TOTAL, 0.3, 0.0005)


def draw_gain(key, part):
    subkeys = jax.random.split(jax.random.fold_in(key, 33), 2)
    diagonal = jnp.exp(jax.random.uniform(subkeys[0], (STATE,), jnp.float32, math.log(0.05), math.log(0.2)))
    scatter_part = jax.random.uniform(subkeys[1], (STATE, STATE), jnp.float32, -0.002, 0.002)
    return jnp.diag(diagonal) + 0.5 * (scatter_part + jnp.transpose(scatter_part))


def draw_rows_float(key, part):
    subkeys = jax.random.split(jax.random.fold_in(key, 44), 3)
    extent = (CAP, DEVS, DEVS)
    readings = jnp.clip(jax.random.normal(subkeys[0], extent, jnp.float32), -6.0, 6.0)
    coefficients = jax.random.uniform(subkeys[2], (4,) + extent, jnp.float32, -0.7, 0.7)
    precisions = jnp.exp(jax.random.uniform(subkeys[1], extent, jnp.float32, math.log(0.5), math.log(2.0)))
    return jnp.concatenate([readings[None], precisions[None], coefficients], axis=0)


def draw_rows_index(key, part):
    subkeys = jax.random.split(jax.random.fold_in(key, 55), 3)
    extent = (CAP, DEVS, DEVS)
    chosen = jax.random.randint(subkeys[0], extent, 0, 3 * STEPS_DEV)
    step_part = jnp.where(chosen < 2 * STEPS_DEV, chosen % STEPS_DEV, STEPS_DEV)
    owner_ids = jnp.arange(DEVS, dtype=jnp.int32)
    owner_base = jax.random.randint(subkeys[1], (DEVS,), 0, BLOCKS)
    owner_base = jnp.where(owner_ids == 0, BLOCKS - 1, owner_base)
    offsets = jax.random.randint(subkeys[2], extent, 0, 16)
    first_slot = (jnp.arange(CAP)[:, None, None] == 0) & (jnp.arange(DEVS)[None, :, None] == 0) & (owner_ids[None, None, :] == 0)
    offsets = jnp.where(first_slot, 0, offsets)
    block_part = (owner_base[None, None, :] + offsets) % BLOCKS
    return jnp.stack([step_part, block_part]).astype(jnp.int32)


def noise(own_key, shape, scale, limit, held_as=jnp.bfloat16):
    return jnp.clip(scale * jax.random.normal(own_key, shape, jnp.float32), -limit, limit).astype(held_as)


def setup_inputs(seed: int = 0, part: int = 0) -> dict:
    arg_keys = jax.random.split(jax.random.key(seed), 7)
    own_keys = jax.random.split(jax.random.fold_in(arg_keys[6], part), 7)
    transition = draw_transition(jax.random.fold_in(arg_keys[6], 71), part)
    gain = draw_gain(jax.random.fold_in(arg_keys[6], 71), part)
    smoother_gain = draw_smoother_gain(jax.random.fold_in(arg_keys[6], 71), part)
    start_state = noise(own_keys[3], (STATE,), 1.0, 6.0, jnp.float32)
    rows_float = draw_rows_float(jax.random.fold_in(jax.random.fold_in(arg_keys[6], part), 71), part)
    rows_index = draw_rows_index(jax.random.fold_in(jax.random.fold_in(arg_keys[6], part), 71), part)
    return dict(transition=transition, gain=gain, smoother_gain=smoother_gain, start_state=start_state, rows_float=rows_float, rows_index=rows_index)


highest = lax.Precision.HIGHEST


def product(matrix_a, matrix_b):
    return jnp.dot(matrix_a, matrix_b, precision=highest, preferred_element_type=jnp.float32)


def reference(transition, gain, smoother_gain, start_state, rows_float, rows_index):
    owner_float = jnp.transpose(rows_float, (3, 0, 1, 2)).reshape(DEVS, 6, CAP * DEVS)
    owner_index = jnp.transpose(rows_index, (3, 0, 1, 2)).reshape(DEVS, 2, CAP * DEVS)
    block_ids = jnp.arange(STATE // 4, dtype=jnp.int32)
    step_ids = jnp.arange(STEPS_DEV, dtype=jnp.int32)

    def owner_pass(estimate, owned):
        floats, integers = owned
        readings = floats[0]
        precision_w = floats[1]
        coefficients = floats[2:]
        member = (integers[1][:, None] == block_ids[None, :]).astype(jnp.float32)
        design = (member[:, :, None] * jnp.transpose(coefficients)[:, None, :]).reshape(-1, STATE)
        chosen = (integers[0][None, :] == step_ids[:, None]).astype(jnp.float32) * precision_w[None, :]

        def one_step(previous, chosen_row):
            predicted = product(transition, previous)
            mismatch = readings - product(design, predicted)
            updated = predicted + product(gain, product(chosen_row * mismatch, design))
            return updated, updated

        return lax.scan(one_step, estimate, chosen)

    _, filtered = lax.scan(owner_pass, start_state.astype(jnp.float32), (owner_float, owner_index))
    filtered = filtered.reshape(TOTAL, STATE)

    def back_step(following, current):
        smoothed_now = current + product(smoother_gain, following - product(transition, current))
        return smoothed_now, smoothed_now

    _, earlier_rows = lax.scan(back_step, filtered[-1], filtered[:-1], reverse=True)
    smoothed = jnp.concatenate([earlier_rows, filtered[-1:]], axis=0)
    return filtered, smoothed
```

```python
import functools
import jax
import jax.numpy as jnp
from jax import lax
from jax.experimental import pallas as pl
from jax.experimental.pallas import tpu as pltpu
from jax.sharding import PartitionSpec as P

STEPS_DEV = 4


highest = lax.Precision.HIGHEST


def entering(value, axis, join, neutral, backward):
    count, mine = (lax.axis_size(axis), lax.axis_index(axis))
    pieces = jax.tree.map(lambda part: lax.all_gather(part, axis), value)
    if backward:
        pieces = jax.tree.map(lambda part: part[::-1], pieces)
        mine = count - 1 - mine
    total = jax.tree.map(
        lambda part, zero: jnp.full_like(part, 0) + jnp.asarray(zero, part.dtype), value, neutral
    )

    def turn(position, total):
        longer = join(total, jax.tree.map(lambda part: part[position], pieces))
        return jax.tree.map(lambda new, old: jnp.where(position < mine, new, old), longer, total)

    return lax.fori_loop(0, count - 1, turn, total)


def from_root(shard, axis, root):
    mine = lax.axis_index(axis) == root
    return lax.psum(jnp.where(mine, shard, jnp.zeros_like(shard)), axis)


def product(matrix_a, matrix_b):
    return jnp.dot(matrix_a, matrix_b, precision=highest, preferred_element_type=jnp.float32)


def chain_link(earlier, later):
    return (product(later[0], earlier[0]), product(later[0], earlier[1]) + later[1])


def on_device(transition, gain, smoother_gain, start_state, rows_float, rows_index):
    received_float = lax.all_to_all(
        rows_float, ("tm", "ingest"), split_axis=3, concat_axis=2, tiled=True
    )
    received_index = lax.all_to_all(
        rows_index, ("tm", "ingest"), split_axis=3, concat_axis=2, tiled=True
    )
    states = transition.shape[0]
    blocks = states // 4
    values = received_float.reshape(6, -1)
    indices = received_index.reshape(2, -1)
    slot_total = values.shape[1]
    readings = values[0]
    precisions = values[1]
    coefficients = values[2:]
    onehot = (indices[1][:, None] == jnp.arange(blocks, dtype=jnp.int32)[None, :]).astype(
        jnp.float32
    )
    design = (onehot[:, :, None] * jnp.transpose(coefficients)[:, None, :]).reshape(
        slot_total, states
    )
    design_next = product(design, transition)
    spread = product(gain, jnp.transpose(design))
    step_ids = jnp.arange(STEPS_DEV, dtype=jnp.int32)
    select = (indices[0][None, :] == step_ids[:, None]).astype(jnp.float32) * precisions[None, :]
    inflow = product(select * readings[None, :], jnp.transpose(spread))
    identity = jnp.eye(states, dtype=jnp.float32)
    empty_vector = jnp.zeros((states,), jnp.float32)
    inner_count = lax.axis_size("ingest")

    def element_step(element, inputs):
        select_row, inflow_row = inputs
        step_matrix = transition - product(spread * select_row[None, :], design_next)
        return (
            (product(step_matrix, element[0]), product(step_matrix, element[1]) + inflow_row),
            None,
        )

    (block_map, block_offset), _ = lax.scan(
        element_step, (identity, empty_vector), (select, inflow)
    )
    inner_before = entering(
        (block_map, block_offset), "ingest", chain_link, (identity, empty_vector), False
    )
    inner_through = chain_link(inner_before, (block_map, block_offset))
    group_map, group_offset = (
        from_root(inner_through[0], "ingest", inner_count - 1),
        from_root(inner_through[1], "ingest", inner_count - 1),
    )
    outer_before = entering(
        (group_map, group_offset), "tm", chain_link, (identity, empty_vector), False
    )
    before_map, before_offset = chain_link(outer_before, inner_before)
    state_entry = product(before_map, start_state) + before_offset

    def filter_step(previous, inputs):
        select_row, inflow_row = inputs
        updated = (
            product(transition, previous)
            - product(spread, select_row * product(design_next, previous))
            + inflow_row
        )
        return (updated, updated)

    _, filtered = lax.scan(filter_step, state_entry, (select, inflow))
    position = lax.axis_index(("tm", "ingest"))
    device_count = lax.axis_size(("tm", "ingest"))
    pushed = product(product(filtered, jnp.transpose(transition)), jnp.transpose(smoother_gain))
    final_row = (position == device_count - 1) & (step_ids == STEPS_DEV - 1)
    residue = filtered - jnp.where(final_row[:, None], 0.0, pushed)

    def tail_step(running, residue_row):
        return (product(smoother_gain, running) + residue_row, None)

    tail_offset, _ = lax.scan(tail_step, empty_vector, residue, reverse=True)
    gain_power = lax.fori_loop(
        0, STEPS_DEV - 1, lambda turn, current: product(smoother_gain, current), smoother_gain
    )
    later_inner = entering(
        (gain_power, tail_offset), "ingest", chain_link, (identity, empty_vector), True
    )
    later_through = chain_link(later_inner, (gain_power, tail_offset))
    later_group = (
        from_root(later_through[0], "ingest", 0),
        from_root(later_through[1], "ingest", 0),
    )
    later_outer = entering(later_group, "tm", chain_link, (identity, empty_vector), True)
    _, smooth_entry = chain_link(later_outer, later_inner)

    def smooth_step(following, residue_row):
        current = product(smoother_gain, following) + residue_row
        return (current, current)

    _, smoothed = lax.scan(smooth_step, smooth_entry, residue, reverse=True)
    return (filtered, smoothed)


bf16 = jnp.bfloat16
f32 = jnp.float32
TRANSPOSED = (((1,), (1,)), ((), ()))


def split(value):
    high = value.astype(bf16)
    return high, (value - high.astype(f32)).astype(bf16)


def mul(left, right, dims=(((1,), (0,)), ((), ()))):
    def one(a, b):
        return lax.dot_general(a, b, dims, preferred_element_type=f32)

    return one(left[0], right[0]) + (one(left[0], right[1]) + one(left[1], right[0]))


def kernel(owners, a_ref, g_ref, s_ref, x0_ref, cols_ref, rows_ref, filt_ref, smooth_ref, bank, small, x_buf, z_buf):
    states = a_ref.shape[0]
    slots = rows_ref.shape[1]
    per_owner = slots // owners
    tile = 4 * per_owner
    supers = owners // 4
    steps = owners * STEPS_DEV
    span = 4 * STEPS_DEV
    position = lax.axis_index("tm") * lax.axis_size("ingest") + lax.axis_index("ingest")

    def put(k, value):
        high, low = split(value)
        bank[k, 0] = high
        bank[k, 1] = low

    def get(k):
        return bank[k, 0], bank[k, 1]

    A, A2, A4, A8, AT, A2T, A4T, A8T, GT, AGT, ST, ST2, ST4, ST8, ST16, ST32, H, PA, RA = range(19)
    a = a_ref[...]
    put(A, a)
    put(AT, a.T)
    put(GT, g_ref[...].T)
    put(ST, s_ref[...].T)
    for src, dst, dst_t in ((A, A2, A2T), (A2, A4, A4T), (A4, A8, A8T)):
        value = mul(get(src), get(src))
        put(dst, value)
        put(dst_t, value.T)
    put(AGT, mul(get(GT), get(AT)))
    for src, dst in ((ST, ST2), (ST2, ST4), (ST4, ST8), (ST8, ST16), (ST16, ST32)):
        put(dst, mul(get(src), get(src)))

    cols = cols_ref[...]
    step_col = cols[:, 6:7].astype(jnp.int32)
    used_col = step_col < STEPS_DEV
    weight_col = jnp.where(used_col, cols[:, 1:2], 0.0)
    step_col = jnp.where(used_col, step_col, 0)
    block_col = cols[:, 7:8].astype(jnp.int32)
    lane = lax.broadcasted_iota(jnp.int32, (slots, states), 1)
    k = lane & 3
    pattern = jnp.where(
        k == 0,
        cols[:, 2:3],
        jnp.where(k == 1, cols[:, 3:4], jnp.where(k == 2, cols[:, 4:5], cols[:, 5:6])),
    )
    design = jnp.where((lane >> 2) == block_col, pattern, 0.0)
    put(H, design)
    put(PA, design)
    put(RA, mul(get(H), get(AGT)) * weight_col)

    owner_col = lax.broadcasted_iota(jnp.int32, (slots, 1), 0) // per_owner
    tau_col = (owner_col % 4) * STEPS_DEV + step_col
    row_values = rows_ref[...]
    step_row = row_values[6:7].astype(jnp.int32)
    used_row = step_row < STEPS_DEV
    weight_row = jnp.where(used_row, row_values[1:2], 0.0)
    step_row = jnp.where(used_row, step_row, 0)
    owner_row = lax.broadcasted_iota(jnp.int32, (1, slots), 1) // per_owner
    tau_row = (owner_row % 4) * STEPS_DEV + step_row

    inverse = [None] * supers
    for level, (power, power_t) in enumerate(((A, AT), (A2, A2T), (A4, A4T), (A8, A8T))):
        p, r = get(PA), get(RA)
        for q in range(supers):
            part = slice(q * tile, (q + 1) * tile)
            gram = mul((p[0][part], p[1][part]), (r[0][part], r[1][part]), TRANSPOSED)
            tc, tr = tau_col[part], tau_row[:, part]
            keep = ((tc >> (level + 1)) == (tr >> (level + 1))) & (((tc >> level) & 1) == 1)
            keep = keep & (((tr >> level) & 1) == 0)
            gram = jnp.where(keep, gram, 0.0)
            if level == 0:
                eye = lax.broadcasted_iota(jnp.int32, (tile, tile), 0) == lax.broadcasted_iota(
                    jnp.int32, (tile, tile), 1
                )
                inverse[q] = eye.astype(f32) - gram
            else:
                t = split(inverse[q])
                inverse[q] = inverse[q] - mul(t, split(mul(split(gram), t)))
        bit_col = ((tau_col >> level) & 1) == 1
        moved_p = mul(p, get(power))
        moved_r = mul(r, get(power_t))
        old_p = p[0].astype(f32) + p[1].astype(f32)
        old_r = r[0].astype(f32) + r[1].astype(f32)
        put(PA, jnp.where(bit_col, moved_p, old_p))
        put(RA, jnp.where(bit_col, old_r, moved_r))

    readings = []
    p = get(PA)
    for q in range(supers):
        part = slice(q * tile, (q + 1) * tile)
        t = split(inverse[q])
        seen = mul(t, (p[0][part], p[1][part]))
        high, low = split(seen.T)
        small[q, 0] = high
        small[q, 1] = low
        y = jnp.broadcast_to(row_values[0:1, part], (16, tile))
        readings.append(mul(split(y), t, TRANSPOSED))

    state = jnp.broadcast_to(x0_ref[...], (16, states))
    state = mul(split(state), get(AT))
    starts, innovations = [], []
    for q in range(supers):
        part = slice(q * tile, (q + 1) * tile)
        starts.append(state)
        parts = split(state)
        innovation = readings[q] - mul(parts, (small[q, 0], small[q, 1]))
        innovations.append(innovation)
        if q + 1 < supers:
            half = mul(parts, get(A8T))
            state = mul(split(half), get(A8T)) + mul(
                split(innovation), (bank[RA, 0, part], bank[RA, 1, part])
            )
    innovation = jnp.concatenate([part[0:1] for part in innovations], axis=1)
    times = lax.broadcasted_iota(jnp.int32, (steps, 1), 0)
    here = lax.broadcasted_iota(jnp.int32, (steps, slots), 0) == owner_row * STEPS_DEV + step_row
    pushes = jnp.where(here, innovation * weight_row, 0.0)
    pushed = split(mul(split(pushes), get(H)))
    predicted = pltpu.roll(mul(pushed, get(AGT)), 1, 0)
    for q in range(supers):
        predicted = jnp.where(times == q * span, starts[q][0:1], predicted)
    for level, power_t in enumerate((AT, A2T, A4T, A8T)):
        reach = 1 << level
        earlier = jnp.where(times % span >= reach, pltpu.roll(predicted, reach, 0), 0.0)
        predicted = predicted + mul(split(earlier), get(power_t))
    filtered = predicted + mul(pushed, get(GT))
    x_buf[...] = filtered
    following = jnp.where(times < steps - 1, pltpu.roll(predicted, steps - 1, 0), 0.0)
    smoothed = filtered - mul(split(following), get(ST))
    for level, power_t in enumerate((ST, ST2, ST4, ST8, ST16, ST32)):
        reach = 1 << level
        later = jnp.where(times < steps - reach, pltpu.roll(smoothed, steps - reach, 0), 0.0)
        smoothed = smoothed + mul(split(later), get(power_t))
    z_buf[...] = smoothed
    base = pl.ds(pl.multiple_of(position // 2 * 8, 8), 8)
    upper = position % 2 == 1
    for buf, out_ref in ((x_buf, filt_ref), (z_buf, smooth_ref)):
        pair = buf[base, :]
        out_ref[...] = jnp.where(upper, pair[4:8], pair[0:4])


def whole_window(transition, gain, smoother_gain, start_state, rows_float, rows_index):
    states = transition.shape[0]
    fields = jnp.concatenate([rows_float, rows_index.astype(f32)], axis=0)
    fields = lax.all_gather(fields, ("tm", "ingest"), axis=2, tiled=True)
    owners = fields.shape[3]
    rows = jnp.transpose(fields, (0, 3, 1, 2)).reshape(8, -1)
    cols = jnp.transpose(rows)
    slots = rows.shape[1]
    tile = slots // owners * 4
    vmem = pl.BlockSpec(memory_space=pltpu.VMEM)
    return pl.pallas_call(
        functools.partial(kernel, owners),
        out_shape=[jax.ShapeDtypeStruct((STEPS_DEV, states), f32)] * 2,
        in_specs=[vmem] * 6,
        out_specs=[vmem] * 2,
        scratch_shapes=[
            pltpu.VMEM((19, 2, states, states), bf16),
            pltpu.VMEM((owners // 4, 2, states, tile), bf16),
            pltpu.VMEM((owners * STEPS_DEV, states), f32),
            pltpu.VMEM((owners * STEPS_DEV, states), f32),
        ],
        compiler_params=pltpu.CompilerParams(vmem_limit_bytes=56 * 1024 * 1024),
    )(transition, gain, smoother_gain, start_state[None], cols, rows)


def on_one(*args):
    owners = args[4].shape[3]
    if owners == 16 and args[4].shape[1] * owners == 32:
        return whole_window(*args)
    return on_device(*args)


def solution(mesh):
    placed = (
        P(),
        P(),
        P(),
        P("groups"),
        P(None, None, ("groups", "tm", "ingest"), None),
        P(None, None, ("groups", "tm", "ingest"), None),
    )
    return jax.shard_map(
        on_one,
        mesh=mesh,
        in_specs=placed,
        out_specs=(P(("groups", "tm", "ingest"), None), P(("groups", "tm", "ingest"), None)),
        check_vma=False,
    )
```

```python
import functools
import jax
import jax.numpy as jnp
from jax import lax
from jax.experimental import pallas as pl
from jax.experimental.pallas import tpu as pltpu
from jax.sharding import PartitionSpec as P

STEPS_DEV = 4


highest = lax.Precision.HIGHEST


def entering(value, axis, join, neutral, backward):
    count, mine = (lax.axis_size(axis), lax.axis_index(axis))
    pieces = jax.tree.map(lambda part: lax.all_gather(part, axis), value)
    if backward:
        pieces = jax.tree.map(lambda part: part[::-1], pieces)
        mine = count - 1 - mine
    total = jax.tree.map(
        lambda part, zero: jnp.full_like(part, 0) + jnp.asarray(zero, part.dtype), value, neutral
    )

    def turn(position, total):
        longer = join(total, jax.tree.map(lambda part: part[position], pieces))
        return jax.tree.map(lambda new, old: jnp.where(position < mine, new, old), longer, total)

    return lax.fori_loop(0, count - 1, turn, total)


def from_root(shard, axis, root):
    mine = lax.axis_index(axis) == root
    return lax.psum(jnp.where(mine, shard, jnp.zeros_like(shard)), axis)


def product(matrix_a, matrix_b):
    return jnp.dot(matrix_a, matrix_b, precision=highest, preferred_element_type=jnp.float32)


def chain_link(earlier, later):
    return (product(later[0], earlier[0]), product(later[0], earlier[1]) + later[1])


def on_device(transition, gain, smoother_gain, start_state, rows_float, rows_index):
    received_float = lax.all_to_all(
        rows_float, ("tm", "ingest"), split_axis=3, concat_axis=2, tiled=True
    )
    received_index = lax.all_to_all(
        rows_index, ("tm", "ingest"), split_axis=3, concat_axis=2, tiled=True
    )
    states = transition.shape[0]
    blocks = states // 4
    values = received_float.reshape(6, -1)
    indices = received_index.reshape(2, -1)
    slot_total = values.shape[1]
    readings = values[0]
    precisions = values[1]
    coefficients = values[2:]
    onehot = (indices[1][:, None] == jnp.arange(blocks, dtype=jnp.int32)[None, :]).astype(
        jnp.float32
    )
    design = (onehot[:, :, None] * jnp.transpose(coefficients)[:, None, :]).reshape(
        slot_total, states
    )
    design_next = product(design, transition)
    spread = product(gain, jnp.transpose(design))
    step_ids = jnp.arange(STEPS_DEV, dtype=jnp.int32)
    select = (indices[0][None, :] == step_ids[:, None]).astype(jnp.float32) * precisions[None, :]
    inflow = product(select * readings[None, :], jnp.transpose(spread))
    identity = jnp.eye(states, dtype=jnp.float32)
    empty_vector = jnp.zeros((states,), jnp.float32)
    inner_count = lax.axis_size("ingest")

    def element_step(element, inputs):
        select_row, inflow_row = inputs
        step_matrix = transition - product(spread * select_row[None, :], design_next)
        return (
            (product(step_matrix, element[0]), product(step_matrix, element[1]) + inflow_row),
            None,
        )

    (block_map, block_offset), _ = lax.scan(
        element_step, (identity, empty_vector), (select, inflow)
    )
    inner_before = entering(
        (block_map, block_offset), "ingest", chain_link, (identity, empty_vector), False
    )
    inner_through = chain_link(inner_before, (block_map, block_offset))
    group_map, group_offset = (
        from_root(inner_through[0], "ingest", inner_count - 1),
        from_root(inner_through[1], "ingest", inner_count - 1),
    )
    outer_before = entering(
        (group_map, group_offset), "tm", chain_link, (identity, empty_vector), False
    )
    before_map, before_offset = chain_link(outer_before, inner_before)
    state_entry = product(before_map, start_state) + before_offset

    def filter_step(previous, inputs):
        select_row, inflow_row = inputs
        updated = (
            product(transition, previous)
            - product(spread, select_row * product(design_next, previous))
            + inflow_row
        )
        return (updated, updated)

    _, filtered = lax.scan(filter_step, state_entry, (select, inflow))
    position = lax.axis_index(("tm", "ingest"))
    device_count = lax.axis_size(("tm", "ingest"))
    pushed = product(product(filtered, jnp.transpose(transition)), jnp.transpose(smoother_gain))
    final_row = (position == device_count - 1) & (step_ids == STEPS_DEV - 1)
    residue = filtered - jnp.where(final_row[:, None], 0.0, pushed)

    def tail_step(running, residue_row):
        return (product(smoother_gain, running) + residue_row, None)

    tail_offset, _ = lax.scan(tail_step, empty_vector, residue, reverse=True)
    gain_power = lax.fori_loop(
        0, STEPS_DEV - 1, lambda turn, current: product(smoother_gain, current), smoother_gain
    )
    later_inner = entering(
        (gain_power, tail_offset), "ingest", chain_link, (identity, empty_vector), True
    )
    later_through = chain_link(later_inner, (gain_power, tail_offset))
    later_group = (
        from_root(later_through[0], "ingest", 0),
        from_root(later_through[1], "ingest", 0),
    )
    later_outer = entering(later_group, "tm", chain_link, (identity, empty_vector), True)
    _, smooth_entry = chain_link(later_outer, later_inner)

    def smooth_step(following, residue_row):
        current = product(smoother_gain, following) + residue_row
        return (current, current)

    _, smoothed = lax.scan(smooth_step, smooth_entry, residue, reverse=True)
    return (filtered, smoothed)


bf16 = jnp.bfloat16
f32 = jnp.float32
TRANSPOSED = (((1,), (1,)), ((), ()))


def split(value):
    high = value.astype(bf16)
    return high, (value - high.astype(f32)).astype(bf16)


def mul(left, right, dims=(((1,), (0,)), ((), ()))):
    def one(a, b):
        return lax.dot_general(a, b, dims, preferred_element_type=f32)

    count = left[0].shape[0]
    if count <= 64:
        both = one(jnp.concatenate(left, axis=0), right[0])
        return both[:count] + both[count:] + one(left[0], right[1])
    return one(left[0], right[0]) + (one(left[0], right[1]) + one(left[1], right[0]))


def kernel(
    owners,
    a_hbm,
    g_hbm,
    s_hbm,
    x0_ref,
    float_ref,
    index_ref,
    filt_ref,
    smooth_ref,
    params,
    bank,
    small,
    x_buf,
    z_buf,
    sending,
    arriving,
    load_sem,
    send_sem,
    recv_sem,
):
    states = a_hbm.shape[0]
    cap = float_ref.shape[1]
    slots = owners * owners * cap
    per_owner = slots // owners
    tile = 4 * per_owner
    supers = owners // 4
    steps = owners * STEPS_DEV
    span = 4 * STEPS_DEV
    position = lax.axis_index("tm") * lax.axis_size("ingest") + lax.axis_index("ingest")

    def put(k, value):
        high, low = split(value)
        bank[k, 0] = high
        bank[k, 1] = low

    def get(k):
        return bank[k, 0], bank[k, 1]

    A, A2, A4, A8, AT, A2T, A4T, A8T, GT, AGT, ST, ST2, ST4, ST8, ST16, ST32, H, PA, RA = range(19)
    loads = [
        pltpu.make_async_copy(hbm, params.at[k], load_sem.at[k])
        for k, hbm in enumerate((a_hbm, s_hbm, g_hbm))
    ]
    for load in loads:
        load.start()
    group = lax.axis_index("groups")
    inner = lax.axis_size("ingest")
    peers = []
    for distance in range(1, owners):
        other = lax.rem(position + distance, owners)
        peers.append((group, other // inner, lax.rem(other, inner)))
    barrier = pltpu.get_barrier_semaphore()
    for peer in peers:
        pl.semaphore_signal(barrier, inc=1, device_id=peer, device_id_type=pl.DeviceIdType.MESH)

    fields = [
        jnp.concatenate([float_ref[f, c] for c in range(cap)], axis=1) for f in range(6)
    ] + [
        jnp.concatenate([index_ref[f, c] for c in range(cap)], axis=1).astype(f32)
        for f in range(2)
    ]
    own = jnp.concatenate(fields, axis=0)
    own = jnp.concatenate([own] * 4, axis=1)
    quarter = lax.broadcasted_iota(jnp.int32, own.shape, 1) // per_owner
    own = jnp.where(quarter == position % 4, own, 0.0)
    sending[...] = own
    arriving[position] = own
    pl.semaphore_wait(barrier, owners - 1)
    copies = [
        pltpu.make_async_remote_copy(
            src_ref=sending,
            dst_ref=arriving.at[position],
            send_sem=send_sem.at[k],
            recv_sem=recv_sem.at[k],
            device_id=peer,
            device_id_type=pl.DeviceIdType.MESH,
        )
        for k, peer in enumerate(peers)
    ]
    for copy in copies:
        copy.start()

    loads[0].wait()
    put(A, params[0])
    put(AT, params[0].T)
    for src, dst, dst_t in ((A, A2, A2T), (A2, A4, A4T), (A4, A8, A8T)):
        value = mul(get(src), get(src))
        put(dst, value)
        put(dst_t, value.T)
    loads[1].wait()
    put(ST, params[1].T)
    loads[2].wait()
    put(GT, params[2].T)
    put(AGT, mul(get(GT), get(AT)))
    for src, dst in ((ST, ST2), (ST2, ST4), (ST4, ST8), (ST8, ST16), (ST16, ST32)):
        put(dst, mul(get(src), get(src)))

    for copy in copies:
        copy.wait()
    quads = []
    for q in range(owners // 4):
        quads.append(
            (arriving[4 * q] + arriving[4 * q + 1]) + (arriving[4 * q + 2] + arriving[4 * q + 3])
        )
    mixed = jnp.concatenate(quads, axis=1)
    from_lane = lax.broadcasted_iota(jnp.int32, (slots, slots), 0)
    to_lane = lax.broadcasted_iota(jnp.int32, (slots, slots), 1)
    wanted = (to_lane % per_owner) * owners + to_lane // per_owner
    order = (from_lane == wanted).astype(bf16)
    high, low = split(mixed)
    lowest = (mixed - high.astype(f32) - low.astype(f32)).astype(bf16)
    ordered = jnp.dot(
        jnp.concatenate([high, low, lowest, jnp.zeros_like(high)], axis=0),
        order,
        preferred_element_type=f32,
    )
    row_values = (ordered[0:8] + ordered[8:16]) + ordered[16:24]
    cols = row_values.T
    step_col = cols[:, 6:7].astype(jnp.int32)
    used_col = step_col < STEPS_DEV
    weight_col = jnp.where(used_col, cols[:, 1:2], 0.0)
    step_col = jnp.where(used_col, step_col, 0)
    block_col = cols[:, 7:8].astype(jnp.int32)
    lane = lax.broadcasted_iota(jnp.int32, (slots, states), 1)
    k = lane & 3
    pattern = jnp.where(
        k == 0,
        cols[:, 2:3],
        jnp.where(k == 1, cols[:, 3:4], jnp.where(k == 2, cols[:, 4:5], cols[:, 5:6])),
    )
    design = jnp.where((lane >> 2) == block_col, pattern, 0.0)
    put(H, design)
    put(PA, design)
    put(RA, mul(get(H), get(AGT)) * weight_col)

    owner_col = lax.broadcasted_iota(jnp.int32, (slots, 1), 0) // per_owner
    tau_col = (owner_col % 4) * STEPS_DEV + step_col
    step_row = row_values[6:7].astype(jnp.int32)
    used_row = step_row < STEPS_DEV
    weight_row = jnp.where(used_row, row_values[1:2], 0.0)
    step_row = jnp.where(used_row, step_row, 0)
    owner_row = lax.broadcasted_iota(jnp.int32, (1, slots), 1) // per_owner
    tau_row = (owner_row % 4) * STEPS_DEV + step_row

    inverse = [None] * supers
    for level, (power, power_t) in enumerate(((A, AT), (A2, A2T), (A4, A4T), (A8, A8T))):
        p, r = get(PA), get(RA)
        for q in range(supers):
            part = slice(q * tile, (q + 1) * tile)
            gram = mul((p[0][part], p[1][part]), (r[0][part], r[1][part]), TRANSPOSED)
            tc, tr = tau_col[part], tau_row[:, part]
            keep = ((tc >> (level + 1)) == (tr >> (level + 1))) & (((tc >> level) & 1) == 1)
            keep = keep & (((tr >> level) & 1) == 0)
            gram = jnp.where(keep, gram, 0.0)
            if level == 0:
                eye = lax.broadcasted_iota(jnp.int32, (tile, tile), 0) == lax.broadcasted_iota(
                    jnp.int32, (tile, tile), 1
                )
                inverse[q] = eye.astype(f32) - gram
            else:
                t = split(inverse[q])
                inverse[q] = inverse[q] - mul(t, split(mul(split(gram), t)))
        if level >= 2:
            run = per_owner << (level - 2)

            def pieces(bit):
                return [slice(k * run, (k + 1) * run) for k in range(bit, slots // run, 2)]

            for buf, matrix, bit in ((PA, power, 1), (RA, power_t, 0)):
                chosen = pieces(bit)
                moving = [
                    jnp.concatenate([bank[buf, k, part] for part in chosen], axis=0)
                    for k in range(2)
                ]
                high, low = split(mul(moving, get(matrix)))
                for k, part in enumerate(chosen):
                    bank[buf, 0, part] = high[k * run : (k + 1) * run]
                    bank[buf, 1, part] = low[k * run : (k + 1) * run]
            continue
        bit_col = ((tau_col >> level) & 1) == 1
        moved_p = mul(p, get(power))
        moved_r = mul(r, get(power_t))
        old_p = p[0].astype(f32) + p[1].astype(f32)
        old_r = r[0].astype(f32) + r[1].astype(f32)
        put(PA, jnp.where(bit_col, moved_p, old_p))
        put(RA, jnp.where(bit_col, old_r, moved_r))

    readings = []
    p = get(PA)
    for q in range(supers):
        part = slice(q * tile, (q + 1) * tile)
        t = split(inverse[q])
        seen = mul(t, (p[0][part], p[1][part]))
        high, low = split(seen.T)
        small[q, 0] = high
        small[q, 1] = low
        y = jnp.broadcast_to(row_values[0:1, part], (16, tile))
        readings.append(mul(split(y), t, TRANSPOSED))

    state = jnp.broadcast_to(x0_ref[...], (16, states))
    state = mul(split(state), get(AT))
    starts, innovations = [], []
    for q in range(supers):
        part = slice(q * tile, (q + 1) * tile)
        starts.append(state)
        parts = split(state)
        innovation = readings[q] - mul(parts, (small[q, 0], small[q, 1]))
        innovations.append(innovation)
        if q + 1 < supers:
            half = mul(parts, get(A8T))
            state = mul(split(half), get(A8T)) + mul(
                split(innovation), (bank[RA, 0, part], bank[RA, 1, part])
            )
    innovation = jnp.concatenate([part[0:1] for part in innovations], axis=1)
    times = lax.broadcasted_iota(jnp.int32, (steps, 1), 0)
    here = lax.broadcasted_iota(jnp.int32, (steps, slots), 0) == owner_row * STEPS_DEV + step_row
    pushes = jnp.where(here, innovation * weight_row, 0.0)
    pushed = split(mul(split(pushes), get(H)))
    predicted = pltpu.roll(mul(pushed, get(AGT)), 1, 0)
    for q in range(supers):
        predicted = jnp.where(times == q * span, starts[q][0:1], predicted)
    for level, power_t in enumerate((AT, A2T, A4T, A8T)):
        reach = 1 << level
        earlier = jnp.where(times % span >= reach, pltpu.roll(predicted, reach, 0), 0.0)
        predicted = predicted + mul(split(earlier), get(power_t))
    filtered = predicted + mul(pushed, get(GT))
    x_buf[...] = filtered
    following = jnp.where(times < steps - 1, pltpu.roll(predicted, steps - 1, 0), 0.0)
    smoothed = filtered - mul(split(following), get(ST))
    for level, power_t in enumerate((ST, ST2, ST4, ST8, ST16, ST32)):
        reach = 1 << level
        later = jnp.where(times < steps - reach, pltpu.roll(smoothed, steps - reach, 0), 0.0)
        smoothed = smoothed + mul(split(later), get(power_t))
    z_buf[...] = smoothed
    base = pl.ds(pl.multiple_of(position // 2 * 8, 8), 8)
    upper = position % 2 == 1
    for buf, out_ref in ((x_buf, filt_ref), (z_buf, smooth_ref)):
        pair = buf[base, :]
        out_ref[...] = jnp.where(upper, pair[4:8], pair[0:4])


def whole_window(transition, gain, smoother_gain, start_state, rows_float, rows_index):
    states = transition.shape[0]
    cap, _, owners = rows_float.shape[1:]
    per_owner = cap * owners
    vmem = pl.BlockSpec(memory_space=pltpu.VMEM)
    anywhere = pl.BlockSpec(memory_space=pl.ANY)
    return pl.pallas_call(
        functools.partial(kernel, owners),
        out_shape=[jax.ShapeDtypeStruct((STEPS_DEV, states), f32)] * 2,
        in_specs=[anywhere] * 3 + [vmem] * 3,
        out_specs=[vmem] * 2,
        scratch_shapes=[
            pltpu.VMEM((3, states, states), f32),
            pltpu.VMEM((19, 2, states, states), bf16),
            pltpu.VMEM((owners // 4, 2, states, 4 * per_owner), bf16),
            pltpu.VMEM((owners * STEPS_DEV, states), f32),
            pltpu.VMEM((owners * STEPS_DEV, states), f32),
            pltpu.VMEM((8, 4 * per_owner), f32),
            pltpu.VMEM((owners, 8, 4 * per_owner), f32),
            pltpu.SemaphoreType.DMA((3,)),
            pltpu.SemaphoreType.DMA((owners - 1,)),
            pltpu.SemaphoreType.DMA((owners - 1,)),
        ],
        compiler_params=pltpu.CompilerParams(
            vmem_limit_bytes=56 * 1024 * 1024, collective_id=0, has_side_effects=True
        ),
    )(transition, gain, smoother_gain, start_state[None], rows_float, rows_index)


def on_one(*args):
    owners = args[4].shape[3]
    if owners == 16 and args[4].shape[1] * owners == 32:
        return whole_window(*args)
    return on_device(*args)


def solution(mesh):
    placed = (
        P(),
        P(),
        P(),
        P("groups"),
        P(None, None, ("groups", "tm", "ingest"), None),
        P(None, None, ("groups", "tm", "ingest"), None),
    )
    return jax.shard_map(
        on_one,
        mesh=mesh,
        in_specs=placed,
        out_specs=(P(("groups", "tm", "ingest"), None), P(("groups", "tm", "ingest"), None)),
        check_vma=False,
    )
```

```python
import functools
import jax
import jax.numpy as jnp
from jax import lax
from jax.experimental import pallas as pl
from jax.experimental.pallas import tpu as pltpu
from jax.sharding import PartitionSpec as P

STEPS_DEV = 4


highest = lax.Precision.HIGHEST


def entering(value, axis, join, neutral, backward):
    count, mine = (lax.axis_size(axis), lax.axis_index(axis))
    pieces = jax.tree.map(lambda part: lax.all_gather(part, axis), value)
    if backward:
        pieces = jax.tree.map(lambda part: part[::-1], pieces)
        mine = count - 1 - mine
    total = jax.tree.map(
        lambda part, zero: jnp.full_like(part, 0) + jnp.asarray(zero, part.dtype), value, neutral
    )

    def turn(position, total):
        longer = join(total, jax.tree.map(lambda part: part[position], pieces))
        return jax.tree.map(lambda new, old: jnp.where(position < mine, new, old), longer, total)

    return lax.fori_loop(0, count - 1, turn, total)


def from_root(shard, axis, root):
    mine = lax.axis_index(axis) == root
    return lax.psum(jnp.where(mine, shard, jnp.zeros_like(shard)), axis)


def product(matrix_a, matrix_b):
    return jnp.dot(matrix_a, matrix_b, precision=highest, preferred_element_type=jnp.float32)


def chain_link(earlier, later):
    return (product(later[0], earlier[0]), product(later[0], earlier[1]) + later[1])


def on_device(transition, gain, smoother_gain, start_state, rows_float, rows_index):
    received_float = lax.all_to_all(
        rows_float, ("tm", "ingest"), split_axis=3, concat_axis=2, tiled=True
    )
    received_index = lax.all_to_all(
        rows_index, ("tm", "ingest"), split_axis=3, concat_axis=2, tiled=True
    )
    states = transition.shape[0]
    blocks = states // 4
    values = received_float.reshape(6, -1)
    indices = received_index.reshape(2, -1)
    slot_total = values.shape[1]
    readings = values[0]
    precisions = values[1]
    coefficients = values[2:]
    onehot = (indices[1][:, None] == jnp.arange(blocks, dtype=jnp.int32)[None, :]).astype(
        jnp.float32
    )
    design = (onehot[:, :, None] * jnp.transpose(coefficients)[:, None, :]).reshape(
        slot_total, states
    )
    design_next = product(design, transition)
    spread = product(gain, jnp.transpose(design))
    step_ids = jnp.arange(STEPS_DEV, dtype=jnp.int32)
    select = (indices[0][None, :] == step_ids[:, None]).astype(jnp.float32) * precisions[None, :]
    inflow = product(select * readings[None, :], jnp.transpose(spread))
    identity = jnp.eye(states, dtype=jnp.float32)
    empty_vector = jnp.zeros((states,), jnp.float32)
    inner_count = lax.axis_size("ingest")

    def element_step(element, inputs):
        select_row, inflow_row = inputs
        step_matrix = transition - product(spread * select_row[None, :], design_next)
        return (
            (product(step_matrix, element[0]), product(step_matrix, element[1]) + inflow_row),
            None,
        )

    (block_map, block_offset), _ = lax.scan(
        element_step, (identity, empty_vector), (select, inflow)
    )
    inner_before = entering(
        (block_map, block_offset), "ingest", chain_link, (identity, empty_vector), False
    )
    inner_through = chain_link(inner_before, (block_map, block_offset))
    group_map, group_offset = (
        from_root(inner_through[0], "ingest", inner_count - 1),
        from_root(inner_through[1], "ingest", inner_count - 1),
    )
    outer_before = entering(
        (group_map, group_offset), "tm", chain_link, (identity, empty_vector), False
    )
    before_map, before_offset = chain_link(outer_before, inner_before)
    state_entry = product(before_map, start_state) + before_offset

    def filter_step(previous, inputs):
        select_row, inflow_row = inputs
        updated = (
            product(transition, previous)
            - product(spread, select_row * product(design_next, previous))
            + inflow_row
        )
        return (updated, updated)

    _, filtered = lax.scan(filter_step, state_entry, (select, inflow))
    position = lax.axis_index(("tm", "ingest"))
    device_count = lax.axis_size(("tm", "ingest"))
    pushed = product(product(filtered, jnp.transpose(transition)), jnp.transpose(smoother_gain))
    final_row = (position == device_count - 1) & (step_ids == STEPS_DEV - 1)
    residue = filtered - jnp.where(final_row[:, None], 0.0, pushed)

    def tail_step(running, residue_row):
        return (product(smoother_gain, running) + residue_row, None)

    tail_offset, _ = lax.scan(tail_step, empty_vector, residue, reverse=True)
    gain_power = lax.fori_loop(
        0, STEPS_DEV - 1, lambda turn, current: product(smoother_gain, current), smoother_gain
    )
    later_inner = entering(
        (gain_power, tail_offset), "ingest", chain_link, (identity, empty_vector), True
    )
    later_through = chain_link(later_inner, (gain_power, tail_offset))
    later_group = (
        from_root(later_through[0], "ingest", 0),
        from_root(later_through[1], "ingest", 0),
    )
    later_outer = entering(later_group, "tm", chain_link, (identity, empty_vector), True)
    _, smooth_entry = chain_link(later_outer, later_inner)

    def smooth_step(following, residue_row):
        current = product(smoother_gain, following) + residue_row
        return (current, current)

    _, smoothed = lax.scan(smooth_step, smooth_entry, residue, reverse=True)
    return (filtered, smoothed)


bf16 = jnp.bfloat16
f32 = jnp.float32
TRANSPOSED = (((1,), (1,)), ((), ()))


def split(value):
    high = value.astype(bf16)
    return high, (value - high.astype(f32)).astype(bf16)


def mul(left, right, dims=(((1,), (0,)), ((), ()))):
    def one(a, b):
        return lax.dot_general(a, b, dims, preferred_element_type=f32)

    count = left[0].shape[0]
    if count <= 64:
        both = one(jnp.concatenate(left, axis=0), right[0])
        return both[:count] + both[count:] + one(left[0], right[1])
    return one(left[0], right[0]) + (one(left[0], right[1]) + one(left[1], right[0]))


def kernel(
    owners,
    a_hbm,
    g_hbm,
    s_hbm,
    x0_ref,
    float_ref,
    index_ref,
    out_ref,
    params,
    bank,
    small,
    x_buf,
    z_buf,
    sending,
    arriving,
    load_sem,
    send_sem,
    recv_sem,
):
    states = a_hbm.shape[0]
    cap = float_ref.shape[1]
    slots = owners * owners * cap
    per_owner = slots // owners
    tile = 4 * per_owner
    supers = owners // 4
    steps = owners * STEPS_DEV
    span = 4 * STEPS_DEV
    position = lax.axis_index("tm") * lax.axis_size("ingest") + lax.axis_index("ingest")

    def put(k, value):
        high, low = split(value)
        bank[k, 0] = high
        bank[k, 1] = low

    def get(k):
        return bank[k, 0], bank[k, 1]

    A, A2, A4, A8, AT, A2T, A4T, A8T, GT, AGT, ST, ST2, ST4, ST8, ST16, ST32, H, PA, RA = range(19)
    loads = [
        pltpu.make_async_copy(hbm, params.at[k], load_sem.at[k])
        for k, hbm in enumerate((a_hbm, s_hbm, g_hbm))
    ]
    for load in loads:
        load.start()
    group = lax.axis_index("groups")
    inner = lax.axis_size("ingest")
    peers = []
    for distance in range(1, owners):
        other = lax.rem(position + distance, owners)
        peers.append((group, other // inner, lax.rem(other, inner)))
    barrier = pltpu.get_barrier_semaphore()
    for peer in peers:
        pl.semaphore_signal(barrier, inc=1, device_id=peer, device_id_type=pl.DeviceIdType.MESH)

    fields = [
        jnp.concatenate([float_ref[f, c] for c in range(cap)], axis=1) for f in range(6)
    ] + [
        jnp.concatenate([index_ref[f, c] for c in range(cap)], axis=1).astype(f32)
        for f in range(2)
    ]
    own = jnp.concatenate(fields, axis=0)
    own = jnp.concatenate([own] * 4, axis=1)
    quarter = lax.broadcasted_iota(jnp.int32, own.shape, 1) // per_owner
    own = jnp.where(quarter == position % 4, own, 0.0)
    sending[...] = own
    arriving[position] = own
    loads[0].wait()
    put(A, params[0])
    put(AT, params[0].T)
    for src, dst, dst_t in ((A, A2, A2T), (A2, A4, A4T), (A4, A8, A8T)):
        value = mul(get(src), get(src))
        put(dst, value)
        put(dst_t, value.T)
    loads[2].wait()
    put(GT, params[2].T)
    put(AGT, mul(get(GT), get(AT)))
    pl.semaphore_wait(barrier, owners - 1)
    copies = [
        pltpu.make_async_remote_copy(
            src_ref=sending,
            dst_ref=arriving.at[position],
            send_sem=send_sem.at[k],
            recv_sem=recv_sem.at[k],
            device_id=peer,
            device_id_type=pl.DeviceIdType.MESH,
        )
        for k, peer in enumerate(peers)
    ]
    for copy in copies:
        copy.start()

    loads[1].wait()
    put(ST, params[1].T)
    for src, dst in ((ST, ST2), (ST2, ST4), (ST4, ST8), (ST8, ST16), (ST16, ST32)):
        put(dst, mul(get(src), get(src)))

    for copy in copies:
        copy.wait()
    quads = []
    for q in range(owners // 4):
        quads.append(
            (arriving[4 * q] + arriving[4 * q + 1]) + (arriving[4 * q + 2] + arriving[4 * q + 3])
        )
    mixed = jnp.concatenate(quads, axis=1)
    from_lane = lax.broadcasted_iota(jnp.int32, (slots, slots), 0)
    to_lane = lax.broadcasted_iota(jnp.int32, (slots, slots), 1)
    wanted = (to_lane % per_owner) * owners + to_lane // per_owner
    order = (from_lane == wanted).astype(bf16)
    high, low = split(mixed)
    lowest = (mixed - high.astype(f32) - low.astype(f32)).astype(bf16)
    ordered = jnp.dot(
        jnp.concatenate([high, low, lowest, jnp.zeros_like(high)], axis=0),
        order,
        preferred_element_type=f32,
    )
    row_values = (ordered[0:8] + ordered[8:16]) + ordered[16:24]
    cols = row_values.T
    step_col = cols[:, 6:7].astype(jnp.int32)
    used_col = step_col < STEPS_DEV
    weight_col = jnp.where(used_col, cols[:, 1:2], 0.0)
    step_col = jnp.where(used_col, step_col, 0)
    block_col = cols[:, 7:8].astype(jnp.int32)
    lane = lax.broadcasted_iota(jnp.int32, (slots, states), 1)
    k = lane & 3
    pattern = jnp.where(
        k == 0,
        cols[:, 2:3],
        jnp.where(k == 1, cols[:, 3:4], jnp.where(k == 2, cols[:, 4:5], cols[:, 5:6])),
    )
    design = jnp.where((lane >> 2) == block_col, pattern, 0.0)
    put(H, design)
    put(PA, design)
    put(RA, mul(get(H), get(AGT)) * weight_col)

    owner_col = lax.broadcasted_iota(jnp.int32, (slots, 1), 0) // per_owner
    tau_col = owner_col * STEPS_DEV + step_col
    step_row = row_values[6:7].astype(jnp.int32)
    used_row = step_row < STEPS_DEV
    weight_row = jnp.where(used_row, row_values[1:2], 0.0)
    step_row = jnp.where(used_row, step_row, 0)
    owner_row = lax.broadcasted_iota(jnp.int32, (1, slots), 1) // per_owner
    tau_row = owner_row * STEPS_DEV + step_row

    expected = [
        jnp.broadcast_to(cols[k : k + 2 * tile, 0:1], (2 * tile, 128))
        for k in range(0, slots, 2 * tile)
    ]
    for level, (power, power_t) in enumerate(((A, AT), (A2, A2T), (A4, A4T), (A8, A8T))):
        p, r = get(PA), get(RA)
        run = per_owner << max(level - 2, 0)
        chosen = [slice(k * run, (k + 1) * run) for k in range(slots // run)]
        later_runs, earlier_runs = chosen[1::2], chosen[0::2]
        corrections = []
        for pair in range(supers // 2):
            part = slice(pair * 2 * tile, (pair + 1) * 2 * tile)
            p_pair = (p[0][part], p[1][part])
            gram = mul(p_pair, (r[0][part], r[1][part]), TRANSPOSED)
            tc, tr = tau_col[part], tau_row[:, part]
            keep = ((tc >> (level + 1)) == (tr >> (level + 1))) & (((tc >> level) & 1) == 1)
            keep = keep & (((tr >> level) & 1) == 0)
            gram = jnp.where(keep, gram, 0.0)
            links = split(gram)
            expected[pair] = expected[pair] - mul(links, split(expected[pair]))
            if level >= 2:
                local = [slice(k * run, (k + 1) * run) for k in range(1, 2 * tile // run, 2)]
                links = [jnp.concatenate([link[rows] for rows in local], axis=0) for link in links]
            corrections.append(mul(links, p_pair))
        correction = jnp.concatenate(corrections, axis=0)
        if level >= 2:
            for buf, matrix, runs in ((PA, power, later_runs), (RA, power_t, earlier_runs)):
                moving = [
                    jnp.concatenate([bank[buf, k, rows] for rows in runs], axis=0) for k in range(2)
                ]
                moved = mul(moving, get(matrix))
                if buf == PA:
                    moved = moved - correction
                high, low = split(moved)
                for k, rows in enumerate(runs):
                    bank[buf, 0, rows] = high[k * run : (k + 1) * run]
                    bank[buf, 1, rows] = low[k * run : (k + 1) * run]
            continue
        bit_col = ((tau_col >> level) & 1) == 1
        moved_p = mul(p, get(power))
        moved_r = mul(r, get(power_t))
        old_p = p[0].astype(f32) + p[1].astype(f32)
        old_r = r[0].astype(f32) + r[1].astype(f32)
        put(PA, jnp.where(bit_col, moved_p, old_p) - correction)
        put(RA, jnp.where(bit_col, old_r, moved_r))

    readings = []
    expected_row = jnp.concatenate([part.T[0:16] for part in expected], axis=1)
    for q in range(supers):
        part = slice(q * tile, (q + 1) * tile)
        for k in range(2):
            small[q, k] = bank[PA, k, part].T
        readings.append(expected_row[:, part])

    state = jnp.broadcast_to(x0_ref[...], (16, states))
    state = mul(split(state), get(AT))
    starts, innovations = [], []
    for q in range(supers):
        part = slice(q * tile, (q + 1) * tile)
        starts.append(state)
        parts = split(state)
        innovation = readings[q] - mul(parts, (small[q, 0], small[q, 1]))
        innovations.append(innovation)
        if q + 1 < supers:
            half = mul(parts, get(A8T))
            state = mul(split(half), get(A8T)) + mul(
                split(innovation), (bank[RA, 0, part], bank[RA, 1, part])
            )
    innovation = jnp.concatenate([part[0:1] for part in innovations], axis=1)
    times = lax.broadcasted_iota(jnp.int32, (steps, 1), 0)
    here = lax.broadcasted_iota(jnp.int32, (steps, slots), 0) == owner_row * STEPS_DEV + step_row
    pushes = jnp.where(here, innovation * weight_row, 0.0)
    pushed = split(mul(split(pushes), get(H)))
    predicted = pltpu.roll(mul(pushed, get(AGT)), 1, 0)
    for q in range(supers):
        predicted = jnp.where(times == q * span, starts[q][0:1], predicted)
    for level, power_t in enumerate((AT, A2T, A4T, A8T)):
        reach = 1 << level
        earlier = jnp.where(times % span >= reach, pltpu.roll(predicted, reach, 0), 0.0)
        predicted = predicted + mul(split(earlier), get(power_t))
    filtered = predicted + mul(pushed, get(GT))
    x_buf[...] = filtered
    following = jnp.where(times < steps - 1, pltpu.roll(predicted, steps - 1, 0), 0.0)
    smoothed = filtered - mul(split(following), get(ST))
    for level, power_t in enumerate((ST, ST2, ST4, ST8, ST16, ST32)):
        reach = 1 << level
        later = jnp.where(times < steps - reach, pltpu.roll(smoothed, steps - reach, 0), 0.0)
        smoothed = smoothed + mul(split(later), get(power_t))
    z_buf[...] = smoothed
    base = pl.ds(pl.multiple_of(position // 2 * 8, 8), 8)
    upper = position % 2 == 1
    for k, buf in enumerate((x_buf, z_buf)):
        pair = buf[base, :]
        out_ref[k * STEPS_DEV : (k + 1) * STEPS_DEV] = jnp.where(upper, pair[4:8], pair[0:4])


def whole_window(transition, gain, smoother_gain, start_state, rows_float, rows_index):
    states = transition.shape[0]
    cap, _, owners = rows_float.shape[1:]
    per_owner = cap * owners
    vmem = pl.BlockSpec(memory_space=pltpu.VMEM)
    anywhere = pl.BlockSpec(memory_space=pl.ANY)
    both = pl.pallas_call(
        functools.partial(kernel, owners),
        out_shape=jax.ShapeDtypeStruct((2 * STEPS_DEV, states), f32),
        in_specs=[anywhere] * 3 + [vmem] * 3,
        out_specs=vmem,
        scratch_shapes=[
            pltpu.VMEM((3, states, states), f32),
            pltpu.VMEM((19, 2, states, states), bf16),
            pltpu.VMEM((owners // 4, 2, states, 4 * per_owner), bf16),
            pltpu.VMEM((owners * STEPS_DEV, states), f32),
            pltpu.VMEM((owners * STEPS_DEV, states), f32),
            pltpu.VMEM((8, 4 * per_owner), f32),
            pltpu.VMEM((owners, 8, 4 * per_owner), f32),
            pltpu.SemaphoreType.DMA((3,)),
            pltpu.SemaphoreType.DMA((owners - 1,)),
            pltpu.SemaphoreType.DMA((owners - 1,)),
        ],
        compiler_params=pltpu.CompilerParams(
            vmem_limit_bytes=56 * 1024 * 1024, collective_id=0, has_side_effects=True
        ),
    )(transition, gain, smoother_gain, start_state[None], rows_float, rows_index)
    return both[:STEPS_DEV], both[STEPS_DEV:]


def on_one(*args):
    owners = args[4].shape[3]
    if owners == 16 and args[4].shape[1] * owners == 32:
        return whole_window(*args)
    return on_device(*args)


def solution(mesh):
    placed = (
        P(),
        P(),
        P(),
        P("groups"),
        P(None, None, ("groups", "tm", "ingest"), None),
        P(None, None, ("groups", "tm", "ingest"), None),
    )
    return jax.shard_map(
        on_one,
        mesh=mesh,
        in_specs=placed,
        out_specs=(P(("groups", "tm", "ingest"), None), P(("groups", "tm", "ingest"), None)),
        check_vma=False,
    )
```

```python
import functools
import jax
import jax.numpy as jnp
from jax import lax
from jax.experimental import pallas as pl
from jax.experimental.pallas import tpu as pltpu
from jax.sharding import PartitionSpec as P

STEPS_DEV = 4


highest = lax.Precision.HIGHEST


def entering(value, axis, join, neutral, backward):
    count, mine = (lax.axis_size(axis), lax.axis_index(axis))
    pieces = jax.tree.map(lambda part: lax.all_gather(part, axis), value)
    if backward:
        pieces = jax.tree.map(lambda part: part[::-1], pieces)
        mine = count - 1 - mine
    total = jax.tree.map(
        lambda part, zero: jnp.full_like(part, 0) + jnp.asarray(zero, part.dtype), value, neutral
    )

    def turn(position, total):
        longer = join(total, jax.tree.map(lambda part: part[position], pieces))
        return jax.tree.map(lambda new, old: jnp.where(position < mine, new, old), longer, total)

    return lax.fori_loop(0, count - 1, turn, total)


def from_root(shard, axis, root):
    mine = lax.axis_index(axis) == root
    return lax.psum(jnp.where(mine, shard, jnp.zeros_like(shard)), axis)


def product(matrix_a, matrix_b):
    return jnp.dot(matrix_a, matrix_b, precision=highest, preferred_element_type=jnp.float32)


def chain_link(earlier, later):
    return (product(later[0], earlier[0]), product(later[0], earlier[1]) + later[1])


def on_device(transition, gain, smoother_gain, start_state, rows_float, rows_index):
    received_float = lax.all_to_all(
        rows_float, ("tm", "ingest"), split_axis=3, concat_axis=2, tiled=True
    )
    received_index = lax.all_to_all(
        rows_index, ("tm", "ingest"), split_axis=3, concat_axis=2, tiled=True
    )
    states = transition.shape[0]
    blocks = states // 4
    values = received_float.reshape(6, -1)
    indices = received_index.reshape(2, -1)
    slot_total = values.shape[1]
    readings = values[0]
    precisions = values[1]
    coefficients = values[2:]
    onehot = (indices[1][:, None] == jnp.arange(blocks, dtype=jnp.int32)[None, :]).astype(
        jnp.float32
    )
    design = (onehot[:, :, None] * jnp.transpose(coefficients)[:, None, :]).reshape(
        slot_total, states
    )
    design_next = product(design, transition)
    spread = product(gain, jnp.transpose(design))
    step_ids = jnp.arange(STEPS_DEV, dtype=jnp.int32)
    select = (indices[0][None, :] == step_ids[:, None]).astype(jnp.float32) * precisions[None, :]
    inflow = product(select * readings[None, :], jnp.transpose(spread))
    identity = jnp.eye(states, dtype=jnp.float32)
    empty_vector = jnp.zeros((states,), jnp.float32)
    inner_count = lax.axis_size("ingest")

    def element_step(element, inputs):
        select_row, inflow_row = inputs
        step_matrix = transition - product(spread * select_row[None, :], design_next)
        return (
            (product(step_matrix, element[0]), product(step_matrix, element[1]) + inflow_row),
            None,
        )

    (block_map, block_offset), _ = lax.scan(
        element_step, (identity, empty_vector), (select, inflow)
    )
    inner_before = entering(
        (block_map, block_offset), "ingest", chain_link, (identity, empty_vector), False
    )
    inner_through = chain_link(inner_before, (block_map, block_offset))
    group_map, group_offset = (
        from_root(inner_through[0], "ingest", inner_count - 1),
        from_root(inner_through[1], "ingest", inner_count - 1),
    )
    outer_before = entering(
        (group_map, group_offset), "tm", chain_link, (identity, empty_vector), False
    )
    before_map, before_offset = chain_link(outer_before, inner_before)
    state_entry = product(before_map, start_state) + before_offset

    def filter_step(previous, inputs):
        select_row, inflow_row = inputs
        updated = (
            product(transition, previous)
            - product(spread, select_row * product(design_next, previous))
            + inflow_row
        )
        return (updated, updated)

    _, filtered = lax.scan(filter_step, state_entry, (select, inflow))
    position = lax.axis_index(("tm", "ingest"))
    device_count = lax.axis_size(("tm", "ingest"))
    pushed = product(product(filtered, jnp.transpose(transition)), jnp.transpose(smoother_gain))
    final_row = (position == device_count - 1) & (step_ids == STEPS_DEV - 1)
    residue = filtered - jnp.where(final_row[:, None], 0.0, pushed)

    def tail_step(running, residue_row):
        return (product(smoother_gain, running) + residue_row, None)

    tail_offset, _ = lax.scan(tail_step, empty_vector, residue, reverse=True)
    gain_power = lax.fori_loop(
        0, STEPS_DEV - 1, lambda turn, current: product(smoother_gain, current), smoother_gain
    )
    later_inner = entering(
        (gain_power, tail_offset), "ingest", chain_link, (identity, empty_vector), True
    )
    later_through = chain_link(later_inner, (gain_power, tail_offset))
    later_group = (
        from_root(later_through[0], "ingest", 0),
        from_root(later_through[1], "ingest", 0),
    )
    later_outer = entering(later_group, "tm", chain_link, (identity, empty_vector), True)
    _, smooth_entry = chain_link(later_outer, later_inner)

    def smooth_step(following, residue_row):
        current = product(smoother_gain, following) + residue_row
        return (current, current)

    _, smoothed = lax.scan(smooth_step, smooth_entry, residue, reverse=True)
    return (filtered, smoothed)


bf16 = jnp.bfloat16
f32 = jnp.float32
TRANSPOSED = (((1,), (1,)), ((), ()))


def split(value):
    high = value.astype(bf16)
    return high, (value - high.astype(f32)).astype(bf16)


def mul(left, right, dims=(((1,), (0,)), ((), ()))):
    def one(a, b):
        return lax.dot_general(a, b, dims, preferred_element_type=f32)

    count = left[0].shape[0]
    if count <= 64:
        both = one(jnp.concatenate(left, axis=0), right[0])
        return both[:count] + both[count:] + one(left[0], right[1])
    return one(left[0], right[0]) + (one(left[0], right[1]) + one(left[1], right[0]))


def kernel(
    owners,
    a_hbm,
    g_hbm,
    s_hbm,
    x0_ref,
    float_ref,
    index_ref,
    out_ref,
    params,
    bank,
    small,
    x_buf,
    z_buf,
    sending,
    arriving,
    load_sem,
    send_sem,
    recv_sem,
):
    states = a_hbm.shape[0]
    cap = float_ref.shape[1]
    slots = owners * owners * cap
    per_owner = slots // owners
    tile = 4 * per_owner
    supers = owners // 4
    steps = owners * STEPS_DEV
    span = 4 * STEPS_DEV
    position = lax.axis_index("tm") * lax.axis_size("ingest") + lax.axis_index("ingest")

    def put(k, value):
        high, low = split(value)
        bank[k, 0] = high
        bank[k, 1] = low

    def get(k):
        return bank[k, 0], bank[k, 1]

    A, A2, A4, A8, AT, A2T, A4T, A8T, GT, AGT, ST, ST2, ST4, ST8, H, PA, RA = range(17)
    loads = [
        pltpu.make_async_copy(hbm, params.at[k], load_sem.at[k])
        for k, hbm in enumerate((a_hbm, s_hbm, g_hbm))
    ]
    for load in loads:
        load.start()
    group = lax.axis_index("groups")
    inner = lax.axis_size("ingest")
    peers = []
    for distance in range(1, owners):
        other = lax.rem(position + distance, owners)
        peers.append((group, other // inner, lax.rem(other, inner)))
    barrier = pltpu.get_barrier_semaphore()
    for peer in peers:
        pl.semaphore_signal(barrier, inc=1, device_id=peer, device_id_type=pl.DeviceIdType.MESH)

    fields = [
        jnp.concatenate([float_ref[f, c] for c in range(cap)], axis=1) for f in range(6)
    ] + [
        jnp.concatenate([index_ref[f, c] for c in range(cap)], axis=1).astype(f32)
        for f in range(2)
    ]
    own = jnp.concatenate(fields, axis=0)
    own = jnp.concatenate([own] * 4, axis=1)
    quarter = lax.broadcasted_iota(jnp.int32, own.shape, 1) // per_owner
    own = jnp.where(quarter == position % 4, own, 0.0)
    sending[...] = own
    arriving[position] = own
    loads[0].wait()
    put(A, params[0])
    put(AT, params[0].T)
    for src, dst, dst_t in ((A, A2, A2T), (A2, A4, A4T), (A4, A8, A8T)):
        value = mul(get(src), get(src))
        put(dst, value)
        put(dst_t, value.T)
    pl.semaphore_wait(barrier, owners - 1)
    copies = [
        pltpu.make_async_remote_copy(
            src_ref=sending,
            dst_ref=arriving.at[position],
            send_sem=send_sem.at[k],
            recv_sem=recv_sem.at[k],
            device_id=peer,
            device_id_type=pl.DeviceIdType.MESH,
        )
        for k, peer in enumerate(peers)
    ]
    for copy in copies:
        copy.start()

    loads[2].wait()
    put(GT, params[2].T)
    put(AGT, mul(get(GT), get(AT)))
    loads[1].wait()
    put(ST, params[1].T)
    for src, dst in ((ST, ST2), (ST2, ST4), (ST4, ST8)):
        put(dst, mul(get(src), get(src)))

    for copy in copies:
        copy.wait()
    quads = []
    for q in range(owners // 4):
        quads.append(
            (arriving[4 * q] + arriving[4 * q + 1]) + (arriving[4 * q + 2] + arriving[4 * q + 3])
        )
    mixed = jnp.concatenate(quads, axis=1)
    from_lane = lax.broadcasted_iota(jnp.int32, (slots, slots), 0)
    to_lane = lax.broadcasted_iota(jnp.int32, (slots, slots), 1)
    wanted = (to_lane % per_owner) * owners + to_lane // per_owner
    order = (from_lane == wanted).astype(bf16)
    high, low = split(mixed)
    lowest = (mixed - high.astype(f32) - low.astype(f32)).astype(bf16)
    ordered = jnp.dot(
        jnp.concatenate([high, low, lowest, jnp.zeros_like(high)], axis=0),
        order,
        preferred_element_type=f32,
    )
    row_values = (ordered[0:8] + ordered[8:16]) + ordered[16:24]
    cols = row_values.T
    step_col = cols[:, 6:7].astype(jnp.int32)
    used_col = step_col < STEPS_DEV
    weight_col = jnp.where(used_col, cols[:, 1:2], 0.0)
    step_col = jnp.where(used_col, step_col, 0)
    block_col = cols[:, 7:8].astype(jnp.int32)
    lane = lax.broadcasted_iota(jnp.int32, (slots, states), 1)
    k = lane & 3
    pattern = jnp.where(
        k == 0,
        cols[:, 2:3],
        jnp.where(k == 1, cols[:, 3:4], jnp.where(k == 2, cols[:, 4:5], cols[:, 5:6])),
    )
    design = jnp.where((lane >> 2) == block_col, pattern, 0.0)
    put(H, design)
    put(PA, design)
    put(RA, mul(get(H), get(AGT)) * weight_col)

    owner_col = lax.broadcasted_iota(jnp.int32, (slots, 1), 0) // per_owner
    tau_col = owner_col * STEPS_DEV + step_col
    step_row = row_values[6:7].astype(jnp.int32)
    used_row = step_row < STEPS_DEV
    weight_row = jnp.where(used_row, row_values[1:2], 0.0)
    step_row = jnp.where(used_row, step_row, 0)
    owner_row = lax.broadcasted_iota(jnp.int32, (1, slots), 1) // per_owner
    tau_row = owner_row * STEPS_DEV + step_row

    expected = [
        jnp.broadcast_to(cols[k : k + 2 * tile, 0:1], (2 * tile, 128))
        for k in range(0, slots, 2 * tile)
    ]
    for level, (power, power_t) in enumerate(((A, AT), (A2, A2T), (A4, A4T), (A8, A8T))):
        p, r = get(PA), get(RA)
        run = per_owner << max(level - 2, 0)
        chosen = [slice(k * run, (k + 1) * run) for k in range(slots // run)]
        later_runs, earlier_runs = chosen[1::2], chosen[0::2]
        corrections = []
        for pair in range(supers // 2):
            part = slice(pair * 2 * tile, (pair + 1) * 2 * tile)
            p_pair = (p[0][part], p[1][part])
            gram = mul(p_pair, (r[0][part], r[1][part]), TRANSPOSED)
            tc, tr = tau_col[part], tau_row[:, part]
            keep = ((tc >> (level + 1)) == (tr >> (level + 1))) & (((tc >> level) & 1) == 1)
            keep = keep & (((tr >> level) & 1) == 0)
            gram = jnp.where(keep, gram, 0.0)
            links = split(gram)
            expected[pair] = expected[pair] - mul(links, split(expected[pair]))
            if level >= 2:
                local = [slice(k * run, (k + 1) * run) for k in range(1, 2 * tile // run, 2)]
                links = [jnp.concatenate([link[rows] for rows in local], axis=0) for link in links]
            corrections.append(mul(links, p_pair))
        correction = jnp.concatenate(corrections, axis=0)
        if level >= 2:
            for buf, matrix, runs in ((PA, power, later_runs), (RA, power_t, earlier_runs)):
                moving = [
                    jnp.concatenate([bank[buf, k, rows] for rows in runs], axis=0) for k in range(2)
                ]
                moved = mul(moving, get(matrix))
                if buf == PA:
                    moved = moved - correction
                high, low = split(moved)
                for k, rows in enumerate(runs):
                    bank[buf, 0, rows] = high[k * run : (k + 1) * run]
                    bank[buf, 1, rows] = low[k * run : (k + 1) * run]
            continue
        bit_col = ((tau_col >> level) & 1) == 1
        moved_p = mul(p, get(power))
        moved_r = mul(r, get(power_t))
        old_p = p[0].astype(f32) + p[1].astype(f32)
        old_r = r[0].astype(f32) + r[1].astype(f32)
        put(PA, jnp.where(bit_col, moved_p, old_p) - correction)
        put(RA, jnp.where(bit_col, old_r, moved_r))

    readings = []
    expected_row = jnp.concatenate([part.T[0:16] for part in expected], axis=1)
    for q in range(supers):
        part = slice(q * tile, (q + 1) * tile)
        for k in range(2):
            small[q, k] = bank[PA, k, part].T
        readings.append(expected_row[:, part])

    state = jnp.broadcast_to(x0_ref[...], (16, states))
    state = mul(split(state), get(AT))
    starts, innovations = [], []
    for q in range(supers):
        part = slice(q * tile, (q + 1) * tile)
        starts.append(state)
        parts = split(state)
        innovation = readings[q] - mul(parts, (small[q, 0], small[q, 1]))
        innovations.append(innovation)
        if q + 1 < supers:
            half = mul(parts, get(A8T))
            state = mul(split(half), get(A8T)) + mul(
                split(innovation), (bank[RA, 0, part], bank[RA, 1, part])
            )
    innovation = jnp.concatenate([part[0:1] for part in innovations], axis=1)
    times = lax.broadcasted_iota(jnp.int32, (steps, 1), 0)
    here = lax.broadcasted_iota(jnp.int32, (steps, slots), 0) == owner_row * STEPS_DEV + step_row
    pushes = jnp.where(here, innovation * weight_row, 0.0)
    pushed = split(mul(split(pushes), get(H)))
    predicted = pltpu.roll(mul(pushed, get(AGT)), 1, 0)
    for q in range(supers):
        predicted = jnp.where(times == q * span, starts[q][0:1], predicted)
    for level, power_t in enumerate((AT, A2T, A4T, A8T)):
        reach = 1 << level
        earlier = jnp.where(times % span >= reach, pltpu.roll(predicted, reach, 0), 0.0)
        predicted = predicted + mul(split(earlier), get(power_t))
    filtered = predicted + mul(pushed, get(GT))
    x_buf[...] = filtered
    following = jnp.where(times < steps - 1, pltpu.roll(predicted, steps - 1, 0), 0.0)
    smoothed = filtered - mul(split(following), get(ST))
    for level, power_t in enumerate((ST, ST2, ST4)):
        reach = 1 << level
        later = jnp.where(times < steps - reach, pltpu.roll(smoothed, steps - reach, 0), 0.0)
        smoothed = smoothed + mul(split(later), get(power_t))
    z_buf[...] = smoothed
    entering_rows = smoothed[steps - 8 :]
    for row in range(steps - 16, -8, -8):
        twice = jnp.concatenate([entering_rows, entering_rows], axis=0)
        entering_rows = smoothed[row : row + 8] + mul(split(twice), get(ST8))[0:8]
        z_buf[row : row + 8, :] = entering_rows
    base = pl.ds(pl.multiple_of(position // 2 * 8, 8), 8)
    upper = position % 2 == 1
    for k, buf in enumerate((x_buf, z_buf)):
        pair = buf[base, :]
        out_ref[k * STEPS_DEV : (k + 1) * STEPS_DEV] = jnp.where(upper, pair[4:8], pair[0:4])


def whole_window(transition, gain, smoother_gain, start_state, rows_float, rows_index):
    states = transition.shape[0]
    cap, _, owners = rows_float.shape[1:]
    per_owner = cap * owners
    vmem = pl.BlockSpec(memory_space=pltpu.VMEM)
    anywhere = pl.BlockSpec(memory_space=pl.ANY)
    both = pl.pallas_call(
        functools.partial(kernel, owners),
        out_shape=jax.ShapeDtypeStruct((2 * STEPS_DEV, states), f32),
        in_specs=[anywhere] * 3 + [vmem] * 3,
        out_specs=vmem,
        scratch_shapes=[
            pltpu.VMEM((3, states, states), f32),
            pltpu.VMEM((17, 2, states, states), bf16),
            pltpu.VMEM((owners // 4, 2, states, 4 * per_owner), bf16),
            pltpu.VMEM((owners * STEPS_DEV, states), f32),
            pltpu.VMEM((owners * STEPS_DEV, states), f32),
            pltpu.VMEM((8, 4 * per_owner), f32),
            pltpu.VMEM((owners, 8, 4 * per_owner), f32),
            pltpu.SemaphoreType.DMA((3,)),
            pltpu.SemaphoreType.DMA((owners - 1,)),
            pltpu.SemaphoreType.DMA((owners - 1,)),
        ],
        compiler_params=pltpu.CompilerParams(
            vmem_limit_bytes=56 * 1024 * 1024, collective_id=0, has_side_effects=True
        ),
    )(transition, gain, smoother_gain, start_state[None], rows_float, rows_index)
    return both[:STEPS_DEV], both[STEPS_DEV:]


def on_one(*args):
    owners = args[4].shape[3]
    if owners == 16 and args[4].shape[1] * owners == 32:
        return whole_window(*args)
    return on_device(*args)


def solution(mesh):
    placed = (
        P(),
        P(),
        P(),
        P("groups"),
        P(None, None, ("groups", "tm", "ingest"), None),
        P(None, None, ("groups", "tm", "ingest"), None),
    )
    return jax.shard_map(
        on_one,
        mesh=mesh,
        in_specs=placed,
        out_specs=(P(("groups", "tm", "ingest"), None), P(("groups", "tm", "ingest"), None)),
        check_vma=False,
    )
```
